512 devices in a mesh: ctx: 64 (over y, z_hi, x, core), tp: 8 (over z_lo).
Axes of the slice: x: 4, y: 4, z: 16 (z_hi: 2, z_lo: 8; z = z_hi * 8 + z_lo), core: 2. Of those that a mesh axis runs over, the one named last changes fastest.
Arguments:
- q_self: bfloat16 [8192, 3072], P('ctx', 'tp'), may hold values from -200 to 200
- k_self: bfloat16 [8192, 3072], P('ctx', 'tp'), may hold values from -6 to 6
- v_self: bfloat16 [8192, 3072], P('ctx', 'tp'), may hold values from -12 to 12
- q_cross: bfloat16 [8192, 3072], P('ctx', 'tp'), may hold values from -200 to 200
- k_text: bfloat16 [256, 3072], P('ctx', 'tp'), may hold values from -6 to 6
- v_text: bfloat16 [256, 3072], P('ctx', 'tp'), may hold values from -12 to 12
- text_len: int32 [1], replicated, may hold values from 64 to 256
- timestep: int32 [1], replicated, may hold values from 0 to 999
- gate_table: float32 [1000, 3072], P(None, 'tp'), may hold values from -4 to 4
Outputs:
- attended: bfloat16 [8192, 3072], P(('ctx', 'tp'))
The draws below stay inside these ranges and needn't reach their ends.
Inputs may be any that keep to these rules, and one draw needn't show every extreme that they name: Text positions from text_len on are padding.
All inputs are finite; a program needn't handle non-finite values.
Results may differ from the reference program's by a relative error of at most 0.0033.
Values may be sent and summed in bfloat16 or wider, within the bound.
A program may use at most 64 MiB of HBM per device.

```python
import jax
import jax.numpy as jnp
from jax import lax

HEADS = 24
HD = 128
TXT = 256
STEPS = 1000
TOKENS = 8192
WIDTH = 3072


def pair_base(key, salt, query_rows, key_rows, width, query_scale, key_low):
    key = jax.random.fold_in(key, salt)
    keys_base = jnp.clip(jax.random.normal(jax.random.fold_in(key, 101), (key_rows, width), jnp.float32), -6.0, 6.0)
    keys_base = keys_base * jax.random.uniform(jax.random.fold_in(key, 103), (key_rows, 1), jnp.float32, key_low, 1.0)
    query_base = jnp.clip(jax.random.normal(jax.random.fold_in(key, 102), (query_rows, width), jnp.float32), -6.0, 6.0)
    return (query_scale * query_base, keys_base)


def draw_q_self(key, part):
    query_base, keys_base = pair_base(key, 201, TOKENS, TOKENS, HEADS * HD, 2.5, 1.0)
    return query_base.astype(jnp.bfloat16)


def draw_k_self(key, part):
    query_base, keys_base = pair_base(key, 201, TOKENS, TOKENS, HEADS * HD, 2.5, 1.0)
    return keys_base.astype(jnp.bfloat16)


def draw_q_cross(key, part):
    query_base, keys_base = pair_base(key, 301, TOKENS, TXT, HEADS * HD, 2.5, 1.0)
    return query_base.astype(jnp.bfloat16)


def draw_k_text(key, part):
    query_base, keys_base = pair_base(key, 301, TOKENS, TXT, HEADS * HD, 2.5, 1.0)
    return keys_base.astype(jnp.bfloat16)


def steps_of(stream_key, shape, cuts, low, high):
    def one(position, shards_of):
        heights = jax.random.uniform(jax.random.fold_in(jax.random.fold_in(stream_key, 6), position), (shards_of,), jnp.float32, low / len(cuts), high / len(cuts))
        return jnp.repeat(jnp.exp(heights), shape[position] // shards_of).reshape((-1,) + (1,) * (len(shape) - position - 1))

    gain = one(*cuts[0])
    for cut in cuts[1:]:
        gain = gain * one(*cut)
    return gain


def gaussian(rng, dims, scale, most, shards=(), kind=jnp.bfloat16):
    drawn = scale * jax.random.normal(rng, dims, jnp.float32)
    if shards:
        drawn = drawn * steps_of(rng, dims, shards, -0.22, 0.18)
    return jnp.clip(drawn, -most, most).astype(kind)


def setup_inputs(seed: int = 0) -> dict:
    arg_keys = jax.random.split(jax.random.key(seed), 10)
    return {
        "q_self": draw_q_self(jax.random.fold_in(arg_keys[9], 71), 0),
        "k_self": draw_k_self(jax.random.fold_in(arg_keys[9], 71), 0),
        "v_self": gaussian(arg_keys[2], (TOKENS, WIDTH), 2.0, 12.0, ((0, 64), (1, 8))),
        "q_cross": draw_q_cross(jax.random.fold_in(arg_keys[9], 71), 0),
        "k_text": draw_k_text(jax.random.fold_in(arg_keys[9], 71), 0),
        "v_text": gaussian(arg_keys[5], (TXT, WIDTH), 2.0, 12.0, ((0, 64), (1, 8))),
        "text_len": jax.random.randint(arg_keys[6], (1,), TXT // 4, TXT + 1).astype(jnp.int32),
        "timestep": jax.random.randint(arg_keys[7], (1,), 0, STEPS).astype(jnp.int32),
        "gate_table": gaussian(arg_keys[8], (STEPS, WIDTH), 1.0, 4.0, ((1, 8),), jnp.float32),
    }


def attend(queries, keys, values, key_bias):
    length = queries.shape[0]
    key_rows = keys.shape[0]
    query_heads = queries.reshape(length, HEADS, HD).transpose(1, 0, 2)
    key_heads = keys.reshape(key_rows, HEADS, HD).transpose(1, 0, 2)
    value_heads = values.reshape(key_rows, HEADS, HD).transpose(1, 0, 2)

    def one_head(pieces):
        query_head, key_head, value_head = pieces
        scores = jnp.dot(query_head, key_head.T, preferred_element_type=jnp.float32) * (HD ** -0.5)
        scores = scores + key_bias[None, :]
        row_max = jnp.max(scores, axis=1, keepdims=True)
        weights = jnp.exp(scores - row_max)
        row_sum = jnp.sum(weights, axis=1, keepdims=True)
        product = jnp.dot(weights.astype(jnp.bfloat16), value_head, preferred_element_type=jnp.float32)
        return product / row_sum

    stacked = lax.map(one_head, (query_heads, key_heads, value_heads))
    return stacked.transpose(1, 0, 2).reshape(length, HEADS * HD)


def reference(q_self, k_self, v_self, q_cross, k_text, v_text, text_len, timestep, gate_table):
    self_out = attend(q_self, k_self, v_self, jnp.zeros((TOKENS,), jnp.float32))
    positions = jnp.arange(TXT, dtype=jnp.int32)
    key_bias = jnp.where(positions < text_len[0], 0.0, -jnp.inf).astype(jnp.float32)
    cross_out = attend(q_cross, k_text, v_text, key_bias)
    gate_row = lax.dynamic_index_in_dim(gate_table, timestep[0], 0, keepdims=False)
    return (gate_row[None, :] * self_out + cross_out).astype(jnp.bfloat16)
```

```python
import jax
import jax.numpy as jnp
from jax import lax
from jax.experimental import pallas as pl
from jax.experimental.pallas import tpu as pltpu
from jax.sharding import PartitionSpec as P

HD = 128
ROWS = 128
NH = 3
NX = 4
NY = 4
NT = 8
CHUNK = ROWS // NT
KEYS = NX * NY * ROWS
SCALE2 = HD ** -0.5 * 1.4426950408889634
MESH_ID = pl.DeviceIdType.MESH
SENDS = 192
RECVS = 96


def kernel(
    text_len, timestep, q_ref, k_ref, v_ref, qc_ref, kt_ref, vt_ref, gate_ref, out_ref,
    kb, vb, qb, qcb, gate, txb, tk, acc, sts, racc, rsts, xs, so, xr, sr, cs, cr, wt, ktv, vtv, grow,
    ssem, rsem, lsem,
):
    ctx = lax.axis_index("ctx")
    zl = lax.axis_index("tp")
    y = ctx // 16
    zh = (ctx // 8) % 2
    x = (ctx // 2) % 4
    c = ctx % 2

    def dev(dy=0, dx=0, flip_z=False, flip_c=False, dz=0):
        yy = (y + dy) % NY
        xx = (x + dx) % NX
        zz = 1 - zh if flip_z else zh
        cc = 1 - c if flip_c else c
        return (((yy * 2 + zz) * 4 + xx) * 2 + cc, (zl + dz) % NT)

    sent = []
    counts = {"s": 0, "r": 0, "l": 0}

    def new(kind, n=1):
        first = counts[kind]
        counts[kind] = first + n
        return first

    def send(src, dst, rs, target):
        cp = pltpu.make_async_remote_copy(
            src_ref=src, dst_ref=dst, send_sem=ssem.at[new("s")], recv_sem=rsem.at[rs],
            device_id=target, device_id_type=MESH_ID,
        )
        cp.start()
        sent.append(cp)

    def arrived(ref, rs):
        pltpu.make_async_copy(ref, ref, rsem.at[rs]).wait()

    def fetch(src, dst):
        cp = pltpu.make_async_copy(src, dst, lsem.at[new("l")])
        cp.start()
        return cp

    def cols(h):
        return pl.ds(h * HD, HD)

    barrier = pltpu.get_barrier_semaphore()
    partners = [dev(dx=d) for d in (1, 2, 3)] + [dev(dy=d) for d in (1, 2, 3)]
    partners += [dev(flip_c=True)]
    partners += [dev(dz=d) for d in range(1, NT)] + [dev(dz=d, flip_z=True) for d in range(NT)]
    for partner in partners:
        pl.semaphore_signal(barrier, inc=1, device_id=partner, device_id_type=MESH_ID)

    local = []
    for h in range(NH):
        local.append(fetch(k_ref.at[:, cols(h)], kb.at[h, y, x]))
        local.append(fetch(v_ref.at[:, cols(h)], vb.at[h, y, x]))
        local.append(fetch(q_ref.at[:, cols(h)], qb.at[0, 0, h]))
    late = [fetch(qc_ref, qcb), fetch(gate_ref, gate)]
    zc = zh * 2 + c
    zo = (1 - zh) * 2 + c
    for cp in (fetch(kt_ref, ktv), fetch(vt_ref, vtv)):
        cp.wait()
    txb[zc] = jnp.concatenate(
        [ktv[...].astype(jnp.float32), vtv[...].astype(jnp.float32)], axis=0
    )
    pl.semaphore_wait(barrier, len(partners))

    sib = dev(flip_c=True)
    across = dev(flip_z=True)

    r_k1 = [[new("r") for d in range(3)] for h in range(NH)]
    r_v1 = [[new("r") for d in range(3)] for h in range(NH)]
    r_k2 = [[new("r") for d in range(2)] for h in range(NH)]
    r_v2 = [[new("r") for d in range(2)] for h in range(NH)]
    r_k3 = [[new("r") for d in range(2)] for h in range(NH)]
    r_v3 = [[new("r") for d in range(2)] for h in range(NH)]
    r_q01 = [new("r") for h in range(NH)]
    r_q10 = [new("r") for h in range(NH)]
    r_q11 = [new("r") for h in range(NH)]
    r_tz, r_ts, r_tzs = new("r"), new("r"), new("r")
    r_t1 = [new("r") for d in range(3)]
    r_t2 = [new("r") for d in range(3)]
    r_t3 = new("r")
    r_acc = [[new("r") for h in range(NH)] for p in range(2)]
    r_sts = [[new("r") for h in range(NH)] for p in range(2)]
    r_x = [[new("r") for h in range(NH)] for p in range(2)]
    r_s = [[new("r") for h in range(NH)] for p in range(2)]
    r_c = new("r")

    def first(h):
        for d in (1, 3, 2):
            send(k_ref.at[:, cols(h)], kb.at[h, y, x], r_k1[h][d - 1], dev(dx=d))
            send(v_ref.at[:, cols(h)], vb.at[h, y, x], r_v1[h][d - 1], dev(dy=d))

    def second(h):
        for d in (1, 2, 3):
            arrived(kb.at[h, y, (x - d + NX) % NX], r_k1[h][d - 1])
            arrived(vb.at[h, (y - d + NY) % NY, x], r_v1[h][d - 1])
        for i, d in ((0, 1), (1, 3)):
            send(kb.at[h, y], kb.at[h, y], r_k2[h][i], dev(dy=d))
            send(vb.at[h, :, x], vb.at[h, :, x], r_v2[h][i], dev(dx=d))

    def relay(h):
        for i, d in ((0, 1), (1, 3)):
            yo = (y - d + NY) % NY
            xo = (x - d + NX) % NX
            half = pl.ds(2 * i, 2)
            arrived(kb.at[h, yo], r_k2[h][i])
            send(kb.at[h, yo, half], kb.at[h, yo, half], r_k3[h][i], dev(dy=d))
            arrived(vb.at[h, :, xo], r_v2[h][i])
            send(vb.at[h, half, xo], vb.at[h, half, xo], r_v3[h][i], dev(dx=d))

    def complete(h):
        yo = (y + 2) % NY
        xo = (x + 2) % NX
        for i in range(2):
            half = pl.ds(2 * i, 2)
            arrived(kb.at[h, yo, half], r_k3[h][i])
            arrived(vb.at[h, half, xo], r_v3[h][i])

    def attend(h, p):
        keys = lambda: kb[h].reshape(KEYS, HD)
        values = lambda: vb[h].reshape(KEYS, HD)

        def body(i, unused):
            o = 1 - i
            scores = lax.dot_general(
                qb[p, o, h], keys(), (((1,), (1,)), ((), ())), preferred_element_type=jnp.float32
            )
            top = jnp.max(scores, axis=1, keepdims=True)
            weights = jnp.exp2((scores - top) * SCALE2)
            total = jnp.sum(weights, axis=1, keepdims=True)
            acc[p, h, o] = jnp.dot(
                weights.astype(jnp.bfloat16), values(), preferred_element_type=jnp.float32
            )
            lane = lax.broadcasted_iota(jnp.int32, (ROWS, HD), 1)
            sts[p, h, o] = jnp.where(lane < HD // 2, top, total)
            return unused

        lax.fori_loop(0, 2, body, 0)
        send(acc.at[p, h, 1], racc.at[p, h], r_acc[p][h], sib)
        send(sts.at[p, h, 1], rsts.at[p, h], r_sts[p][h], sib)

    def merge(h, p):
        arrived(racc.at[p, h], r_acc[p][h])
        arrived(rsts.at[p, h], r_sts[p][h])
        one, two = sts[p, h, 0], rsts[p, h]
        top1, sum1 = one[:, :1], one[:, HD // 2 : HD // 2 + 1]
        top2, sum2 = two[:, :1], two[:, HD // 2 : HD // 2 + 1]
        top = jnp.maximum(top1, top2)
        f1 = jnp.exp2((top1 - top) * SCALE2)
        f2 = jnp.exp2((top2 - top) * SCALE2)
        total = sum1 * f1 + sum2 * f2
        g = grow[:, h * HD : (h + 1) * HD]
        mixed = (acc[p, h, 0] * f1 + racc[p, h] * f2) / total * g
        xs[p, h] = mixed.astype(jnp.bfloat16).reshape(NT, CHUNK, HD)
        lane = lax.broadcasted_iota(jnp.int32, (ROWS, HD), 1)
        flat = jnp.where(lane < HD // 2, top, total).T
        so[p, h] = jnp.concatenate([flat[:1], flat[HD // 2 : HD // 2 + 1]], axis=0)
        for d in range(NT) if p == 1 else range(1, NT):
            target = dev(dz=d, flip_z=p == 1)
            send(xs.at[p, h, (zl + d) % NT], xr.at[p, h, zl], r_x[p][h], target)
            send(so.at[p, h], sr.at[p, h, zl], r_s[p][h], target)
        if p == 0:
            pltpu.make_async_copy(xs.at[p, h, zl], xr.at[p, h, zl], rsem.at[r_x[p][h]]).start()
            pltpu.make_async_copy(so.at[p, h], sr.at[p, h, zl], rsem.at[r_s[p][h]]).start()

    first(0)
    send(txb.at[zc], txb.at[zc], r_tz, across)
    send(txb.at[zc], txb.at[zc], r_ts, sib)
    for h in range(NH):
        send(q_ref.at[:, cols(h)], qb.at[1, 0, h], r_q10[h], across)
        send(q_ref.at[:, cols(h)], qb.at[0, 1, h], r_q01[h], sib)
    first(1)
    for cp in local:
        cp.wait()
    second(0)
    first(2)
    second(1)

    arrived(txb.at[zo], r_tz)
    send(txb.at[zo], txb.at[zo], r_tzs, sib)
    arrived(txb.at[zh * 2 + 1 - c], r_ts)
    arrived(txb.at[(1 - zh) * 2 + 1 - c], r_tzs)
    tiles = [txb[i] for i in range(4)]
    own = jnp.concatenate([jnp.where(c == 0, t[:4], t[4:]) for t in tiles], axis=0)
    tk[c, y, x] = own.astype(jnp.bfloat16)
    for d in (1, 2, 3):
        send(tk.at[c, y, x], tk.at[c, y, x], r_t1[d - 1], dev(dx=d))
    relay(0)
    second(2)
    for d in (1, 2, 3):
        arrived(tk.at[c, y, (x - d + NX) % NX], r_t1[d - 1])
    for d in (1, 2, 3):
        send(tk.at[c, y], tk.at[c, y], r_t2[d - 1], dev(dy=d))
    relay(1)
    for h in range(NH):
        arrived(qb.at[0, 1, h], r_q01[h])
    complete(0)
    attend(0, 0)
    arrived(qb.at[1, 0, 0], r_q10[0])
    send(qb.at[1, 0, 0], qb.at[1, 1, 0], r_q11[0], sib)
    for d in (1, 2, 3):
        arrived(tk.at[c, (y - d + NY) % NY], r_t2[d - 1])
    send(tk.at[c], tk.at[c], r_t3, sib)
    relay(2)
    complete(1)
    attend(1, 0)
    for cp in late:
        cp.wait()
    here = lax.broadcasted_iota(jnp.int32, gate.shape, 0) == timestep[0]
    grow[...] = jnp.sum(jnp.where(here, gate[...], 0.0), axis=0, keepdims=True)
    merge(0, 0)
    arrived(qb.at[1, 1, 0], r_q11[0])
    attend(0, 1)
    merge(1, 0)
    for h in (1, 2):
        arrived(qb.at[1, 0, h], r_q10[h])
        send(qb.at[1, 0, h], qb.at[1, 1, h], r_q11[h], sib)
    merge(0, 1)

    arrived(tk.at[1 - c], r_t3)
    j = lax.broadcasted_iota(jnp.int32, (ROWS, NX * NY * 16), 1)
    jy, jx, jz, jc, jr = j >> 6, (j >> 4) & 3, (j >> 3) & 1, (j >> 2) & 1, j & 3
    position = ((((jy * 2 + jz) * 4 + jx) * 2 + jc) << 2) + jr
    live = position < text_len[0]
    for h in range(NH):
        lanes = slice(h * HD, (h + 1) * HD)
        text_keys = tk[0].reshape(NX * NY * 16, NH * HD)[:, lanes]
        text_values = tk[1].reshape(NX * NY * 16, NH * HD)[:, lanes]
        scores = lax.dot_general(
            qcb[:, lanes], text_keys, (((1,), (1,)), ((), ())), preferred_element_type=jnp.float32
        )
        scores = jnp.where(live, scores, -jnp.inf)
        top = jnp.max(scores, axis=1, keepdims=True)
        weights = jnp.exp2((scores - top) * SCALE2)
        total = jnp.sum(weights, axis=1, keepdims=True)
        product = jnp.dot(
            weights.astype(jnp.bfloat16), text_values, preferred_element_type=jnp.float32
        )
        cs[:, :, lanes] = (product / total).astype(jnp.bfloat16).reshape(NT, CHUNK, HD)
    for d in range(1, NT):
        send(cs.at[(zl + d) % NT], cr.at[zl], r_c, dev(dz=d))
    pltpu.make_async_copy(cs.at[zl], cr.at[zl], rsem.at[r_c]).start()

    arrived(qb.at[1, 1, 1], r_q11[1])
    arrived(qb.at[1, 1, 2], r_q11[2])
    attend(1, 1)
    complete(2)
    attend(2, 1)
    merge(1, 1)
    attend(2, 0)
    merge(2, 1)
    merge(2, 0)

    arrived(cr, r_c)
    for p in range(2):
        for h in range(NH):
            arrived(xr.at[p, h], r_x[p][h])
            arrived(sr.at[p, h], r_s[p][h])
    shares = [[], []]
    for h in range(NH):
        one, two = sr[0, h], sr[1, h]
        top1, sum1, top2, sum2 = one[:, 0], one[:, 1], two[:, 0], two[:, 1]
        top = jnp.maximum(top1, top2)
        part1 = sum1 * jnp.exp2((top1 - top) * SCALE2)
        part2 = sum2 * jnp.exp2((top2 - top) * SCALE2)
        whole = part1 + part2
        shares[0].append(part1 / whole)
        shares[1].append(part2 / whole)
    rows = shares[0] + shares[1]
    table = jnp.concatenate(rows + [jnp.zeros((HD - NT * len(rows), HD), jnp.float32)], axis=0)
    wt[...] = table.T
    mine = wt[pl.ds(pl.multiple_of(zl * CHUNK, CHUNK), CHUNK), :]
    for src in range(NT):
        for h in range(NH):
            i, k = h * NT + src, (NH + h) * NT + src
            joined = xr[0, h, src].astype(jnp.float32) * mine[:, i : i + 1]
            joined = joined + xr[1, h, src].astype(jnp.float32) * mine[:, k : k + 1]
            joined = joined + cr[src, :, h * HD : (h + 1) * HD].astype(jnp.float32)
            lo = (src * NH + h) * HD
            out_ref[:, lo : lo + HD] = joined.astype(jnp.bfloat16)

    for cp in sent:
        cp.wait_send()
    assert counts["s"] <= SENDS and counts["r"] <= RECVS, counts


def local(q_self, k_self, v_self, q_cross, k_text, v_text, text_len, timestep, gate_table):
    bf16, f32 = jnp.bfloat16, jnp.float32
    smem = pl.BlockSpec(memory_space=pltpu.SMEM)
    vmem = pl.BlockSpec(memory_space=pltpu.VMEM)
    hbm = pl.BlockSpec(memory_space=pltpu.HBM)
    return pl.pallas_call(
        kernel,
        out_shape=jax.ShapeDtypeStruct((CHUNK, NT * NH * HD), bf16),
        in_specs=[smem, smem, hbm, hbm, hbm, hbm, hbm, hbm, hbm],
        out_specs=vmem,
        scratch_shapes=[
            pltpu.VMEM((NH, NY, NX, ROWS, HD), bf16),
            pltpu.VMEM((NH, NY, NX, ROWS, HD), bf16),
            pltpu.VMEM((2, 2, NH, ROWS, HD), bf16),
            pltpu.VMEM((ROWS, NH * HD), bf16),
            pltpu.VMEM(gate_table.shape, f32),
            pltpu.VMEM((4, 8, NH * HD), f32),
            pltpu.VMEM((2, NY, NX, 16, NH * HD), bf16),
            pltpu.VMEM((2, NH, 2, ROWS, HD), f32),
            pltpu.VMEM((2, NH, 2, ROWS, HD), f32),
            pltpu.VMEM((2, NH, ROWS, HD), f32),
            pltpu.VMEM((2, NH, ROWS, HD), f32),
            pltpu.VMEM((2, NH, NT, CHUNK, HD), bf16),
            pltpu.VMEM((2, NH, 2, HD), f32),
            pltpu.VMEM((2, NH, NT, CHUNK, HD), bf16),
            pltpu.VMEM((2, NH, NT, 2, HD), f32),
            pltpu.VMEM((NT, CHUNK, NH * HD), bf16),
            pltpu.VMEM((NT, CHUNK, NH * HD), bf16),
            pltpu.VMEM((HD, HD), f32),
            pltpu.VMEM(k_text.shape, bf16),
            pltpu.VMEM(v_text.shape, bf16),
            pltpu.VMEM((1, NH * HD), f32),
            pltpu.SemaphoreType.DMA((SENDS,)),
            pltpu.SemaphoreType.DMA((RECVS,)),
            pltpu.SemaphoreType.DMA((16,)),
        ],
        compiler_params=pltpu.CompilerParams(
            collective_id=0, has_side_effects=True, vmem_limit_bytes=64 * 1024 * 1024
        ),
        name="gated_attention",
    )(text_len, timestep, q_self, k_self, v_self, q_cross, k_text, v_text, gate_table)


def solution(mesh):
    placed = (
        P("ctx", "tp"),
        P("ctx", "tp"),
        P("ctx", "tp"),
        P("ctx", "tp"),
        P("ctx", "tp"),
        P("ctx", "tp"),
        P(),
        P(),
        P(None, "tp"),
    )
    return jax.shard_map(
        local, mesh=mesh, in_specs=placed, out_specs=P(("ctx", "tp"), None), check_vma=False
    )
```

```python
import jax
import jax.numpy as jnp
from jax import lax
from jax.experimental import pallas as pl
from jax.experimental.pallas import tpu as pltpu
from jax.sharding import PartitionSpec as P

HD = 128
ROWS = 128
NH = 3
NX = 4
NY = 4
NT = 8
CHUNK = ROWS // NT
KEYS = NX * NY * ROWS
TEXT = NX * NY * 16
SCALE2 = HD ** -0.5 * 1.4426950408889634
MESH_ID = pl.DeviceIdType.MESH
SENDS = 192
RECVS = 96


def kernel(
    text_len, timestep, q_ref, k_ref, v_ref, qc_ref, kt_ref, vt_ref, gate_ref, out_ref,
    kb, vb, qb, qf, qcb, gate, grow, ktv, vtv, txb, txf, tk, acc, sts, racc, rsts, mst,
    xs, so, xr, sr, cs, cr, ssem, rsem, lsem, near_sem, far_sem,
):
    ctx = lax.axis_index("ctx")
    zl = lax.axis_index("tp")
    y = ctx // 16
    zh = (ctx // 8) % 2
    x = (ctx // 2) % 4
    c = ctx % 2

    def dev(dy=0, dx=0, flip_c=False, dz=0):
        yy = (y + dy) % NY
        xx = (x + dx) % NX
        zz = (zh * NT + zl + dz + 2 * NT) % (2 * NT)
        cc = 1 - c if flip_c else c
        return (((yy * 2 + zz // NT) * 4 + xx) * 2 + cc, zz % NT)

    def owner(d, p):
        return (((y * 2 + (1 - zh if p else zh)) * 4 + x) * 2 + c, (zl + d) % NT)

    sent = []
    counts = {"s": 0, "r": 0, "l": 0}

    def new(kind):
        counts[kind] += 1
        return counts[kind] - 1

    def send(src, dst, rs, target):
        cp = pltpu.make_async_remote_copy(
            src_ref=src, dst_ref=dst, send_sem=ssem.at[new("s")], recv_sem=rsem.at[rs],
            device_id=target, device_id_type=MESH_ID,
        )
        cp.start()
        sent.append(cp)

    def arrived(ref, rs):
        pltpu.make_async_copy(ref, ref, rsem.at[rs]).wait()

    def fetch(src, dst):
        cp = pltpu.make_async_copy(src, dst, lsem.at[new("l")])
        cp.start()
        return cp

    def signal(sem, target):
        pl.semaphore_signal(sem, inc=1, device_id=target, device_id_type=MESH_ID)

    def cols(h):
        return pl.ds(h * HD, HD)

    barrier = pltpu.get_barrier_semaphore()
    partners = [dev(dx=d) for d in (1, 2, 3)] + [dev(dy=d) for d in (1, 2, 3)]
    partners += [dev(flip_c=True)] + [dev(dz=d) for d in (1, -1, 2, -2)]
    for partner in partners:
        signal(barrier, partner)

    small = [fetch(kt_ref, ktv), fetch(vt_ref, vtv)]
    local = []
    for h in range(NH):
        local.append(fetch(k_ref.at[:, cols(h)], kb.at[h, y, x]))
        local.append(fetch(v_ref.at[:, cols(h)], vb.at[h, y, x]))
        local.append(fetch(q_ref.at[:, cols(h)], qb.at[h, 3]))
    late = [fetch(qc_ref, qcb), fetch(gate_ref, gate)]
    zc = zh * 2 + c
    zo = (1 - zh) * 2 + c
    for cp in small:
        cp.wait()
    txb[zc] = jnp.concatenate(
        [ktv[...].astype(jnp.float32), vtv[...].astype(jnp.float32)], axis=0
    )
    pl.semaphore_wait(barrier, len(partners))

    sib = dev(flip_c=True)
    quarter = 4 - 8 * c

    def table(*shape):
        if not shape:
            return new("r")
        return [table(*shape[1:]) for unused in range(shape[0])]

    r_k1, r_v1 = table(NH, 3), table(NH, 3)
    r_k2, r_v2, r_k3, r_v3 = table(NH, 2), table(NH, 2), table(NH, 2), table(NH, 2)
    r_qs, r_qf, r_qx, r_qy = table(NH), table(NH, 2), table(NH, 2), table(NH)
    r_tf, r_tz, r_ts, r_ty, r_t1, r_t2, r_t3 = (
        table(), table(), table(), table(), table(3), table(3), table()
    )
    r_acc, r_sts, r_x, r_s, r_c = table(NH), table(NH), table(2, NH), table(2), table()

    def first(h):
        for d in (1, 3, 2):
            send(k_ref.at[:, cols(h)], kb.at[h, y, x], r_k1[h][d - 1], dev(dx=d))
            send(v_ref.at[:, cols(h)], vb.at[h, y, x], r_v1[h][d - 1], dev(dy=d))

    def second(h):
        for d in (1, 2, 3):
            arrived(kb.at[h, y, (x - d + NX) % NX], r_k1[h][d - 1])
            arrived(vb.at[h, (y - d + NY) % NY, x], r_v1[h][d - 1])
        for i, d in ((0, 1), (1, 3)):
            send(kb.at[h, y], kb.at[h, y], r_k2[h][i], dev(dy=d))
            send(vb.at[h, :, x], vb.at[h, :, x], r_v2[h][i], dev(dx=d))

    def relay(h):
        for i, d in ((0, 1), (1, 3)):
            yo = (y - d + NY) % NY
            xo = (x - d + NX) % NX
            half = pl.ds(2 * i, 2)
            arrived(kb.at[h, yo], r_k2[h][i])
            send(kb.at[h, yo, half], kb.at[h, yo, half], r_k3[h][i], dev(dy=d))
            arrived(vb.at[h, :, xo], r_v2[h][i])
            send(vb.at[h, half, xo], vb.at[h, half, xo], r_v3[h][i], dev(dx=d))

    def complete(h):
        yo = (y + 2) % NY
        xo = (x + 2) % NX
        for i in range(2):
            half = pl.ds(2 * i, 2)
            arrived(kb.at[h, yo, half], r_k3[h][i])
            arrived(vb.at[h, half, xo], r_v3[h][i])

    def cross(h):
        for i, d in ((0, 4), (1, -4)):
            rows = pl.ds(64 * i, 64)
            send(q_ref.at[rows, cols(h)], qf.at[i, h], r_qf[h][i], dev(dz=d))

    def pass_on(h):
        for i, d in ((0, 4), (1, -4)):
            rows = pl.ds(64 * i, 64)
            arrived(qf.at[i, h], r_qf[h][i])
            send(qf.at[i, h], qb.at[h, 2, rows], r_qx[h][i], dev(dz=d))

    def share(h):
        for i in range(2):
            arrived(qb.at[h, 2, pl.ds(64 * i, 64)], r_qx[h][i])
        send(qb.at[h, 2], qb.at[h, 0], r_qy[h], sib)

    def attend(h):
        arrived(qb.at[h, 1], r_qs[h])
        arrived(qb.at[h, 0], r_qy[h])
        scores = lax.dot_general(
            kb[h].reshape(KEYS, HD), qb[h].reshape(4 * ROWS, HD), (((1,), (1,)), ((), ())),
            preferred_element_type=jnp.float32,
        )
        top = jnp.max(scores, axis=0, keepdims=True)
        weights = jnp.exp2((scores - top) * SCALE2)
        total = jnp.sum(weights, axis=0, keepdims=True)
        product = lax.dot_general(
            vb[h].reshape(KEYS, HD), weights.astype(jnp.bfloat16), (((0,), (0,)), ((), ())),
            preferred_element_type=jnp.float32,
        )
        for b in range(4):
            lanes = slice(b * ROWS, (b + 1) * ROWS)
            acc[h, b] = product[:, lanes]
            sts[h, b] = jnp.concatenate([top[:, lanes], total[:, lanes]], axis=0)
        send(acc.at[h, pl.ds(0, 2)], racc.at[h], r_acc[h], sib)
        send(sts.at[h, pl.ds(0, 2)], rsts.at[h], r_sts[h], sib)

    def merge(h):
        arrived(racc.at[h], r_acc[h])
        arrived(rsts.at[h], r_sts[h])
        for p in (1, 0):
            mine, yours = 3 - p, 1 - p
            one, two = sts[h, mine], rsts[h, yours]
            top = jnp.maximum(one[:1], two[:1])
            f1 = jnp.exp2((one[:1] - top) * SCALE2)
            f2 = jnp.exp2((two[:1] - top) * SCALE2)
            total = one[1:] * f1 + two[1:] * f2
            mixed = acc[h, mine] * (f1 / total) + racc[h, yours] * (f2 / total)
            mixed = mixed.T * grow[:, h * HD : (h + 1) * HD]
            xs[p, h] = mixed.astype(jnp.bfloat16).reshape(NT, CHUNK, HD)
            lane = lax.broadcasted_iota(jnp.int32, (NT, HD), 1)
            packed = jnp.zeros((NT, HD), jnp.float32) if h == 0 else mst[p]
            for k, row in ((h, top), (4 + h, total)):
                moved = jnp.broadcast_to(row, (NT, HD))
                moved = pltpu.roll(moved, 0, 1, stride=CHUNK, stride_axis=0)
                moved = pltpu.roll(moved, (k + 1) * CHUNK % HD, 1)
                packed = jnp.where((lane >> 4) == k, moved, packed)
            if h < NH - 1:
                mst[p] = packed
            else:
                for i in range(NT):
                    so[p, NT - 1 - i] = packed[i : i + 1]
            for d in range(1 - p, NT):
                target = owner(d, p)
                to = (zl + d) % NT
                send(xs.at[p, h, to], xr.at[p, h, zl], r_x[p][h], target)
                if h == NH - 1:
                    send(so.at[p, to], sr.at[p, zl], r_s[p], target)
            if p == 0:
                pltpu.make_async_copy(xs.at[0, h, zl], xr.at[0, h, zl], rsem.at[r_x[0][h]]).start()
                if h == NH - 1:
                    pltpu.make_async_copy(so.at[0, zl], sr.at[0, zl], rsem.at[r_s[0]]).start()

    def text_column():
        arrived(txb.at[zo], r_tz)
        send(txb.at[zo], txb.at[zo], r_ty, sib)
        arrived(txb.at[zh * 2 + 1 - c], r_ts)
        arrived(txb.at[(1 - zh) * 2 + 1 - c], r_ty)
        tiles = [txb[i] for i in range(4)]
        own = jnp.concatenate([jnp.where(c == 0, t[:4], t[4:]) for t in tiles], axis=0)
        tk[c, y, x] = own.astype(jnp.bfloat16)
        for d in (1, 2, 3):
            send(tk.at[c, y, x], tk.at[c, y, x], r_t1[d - 1], dev(dx=d))

    def text_plane():
        for d in (1, 2, 3):
            arrived(tk.at[c, y, (x - d + NX) % NX], r_t1[d - 1])
        for d in (1, 2, 3):
            send(tk.at[c, y], tk.at[c, y], r_t2[d - 1], dev(dy=d))

    def text_core():
        for d in (1, 2, 3):
            arrived(tk.at[c, (y - d + NY) % NY], r_t2[d - 1])
        send(tk.at[c], tk.at[c], r_t3, sib)

    def text_attend():
        arrived(tk.at[1 - c], r_t3)
        j = lax.broadcasted_iota(jnp.int32, (ROWS, TEXT), 1)
        jy, jx, jz, jc, jr = j >> 6, (j >> 4) & 3, (j >> 3) & 1, (j >> 2) & 1, j & 3
        position = ((((jy * 2 + jz) * 4 + jx) * 2 + jc) << 2) + jr
        live = position < text_len[0]
        for h in range(NH):
            lanes = slice(h * HD, (h + 1) * HD)
            text_keys = tk[0].reshape(TEXT, NH * HD)[:, lanes]
            text_values = tk[1].reshape(TEXT, NH * HD)[:, lanes]
            scores = lax.dot_general(
                qcb[:, lanes], text_keys, (((1,), (1,)), ((), ())),
                preferred_element_type=jnp.float32,
            )
            scores = jnp.where(live, scores, -jnp.inf)
            top = jnp.max(scores, axis=1, keepdims=True)
            weights = jnp.exp2((scores - top) * SCALE2)
            total = jnp.sum(weights, axis=1, keepdims=True)
            product = jnp.dot(
                weights.astype(jnp.bfloat16), text_values, preferred_element_type=jnp.float32
            )
            cs[:, :, lanes] = (product / total).astype(jnp.bfloat16).reshape(NT, CHUNK, HD)
        for d in range(1, NT):
            send(cs.at[(zl + d) % NT], cr.at[zl], r_c, owner(d, 0))
        pltpu.make_async_copy(cs.at[zl], cr.at[zl], rsem.at[r_c]).start()

    first(0)
    send(txb.at[zc], txb.at[zc], r_ts, sib)
    for d in (2, -2):
        signal(near_sem, dev(dz=d))
    first(1)
    for h in range(NH):
        send(q_ref.at[:, cols(h)], qb.at[h, 1], r_qs[h], sib)
    pl.semaphore_wait(near_sem, 2)
    for d in (4, -4):
        signal(far_sem, dev(dz=d))
    send(txb.at[zc], txf, r_tf, dev(dz=quarter))
    for h in range(NH):
        cross(h)
    for cp in local:
        cp.wait()
    second(0)
    first(2)
    second(1)
    arrived(txf, r_tf)
    came = ((zh * NT + zl - quarter + 2 * NT) % (2 * NT)) // NT * 2 + c
    send(txf, txb.at[came], r_tz, dev(dz=quarter))
    pass_on(0)
    second(2)
    pass_on(1)
    relay(0)
    pass_on(2)
    pl.semaphore_wait(far_sem, 2)
    text_column()
    share(0)
    relay(1)
    text_plane()
    for cp in late:
        cp.wait()
    here = lax.broadcasted_iota(jnp.int32, gate.shape, 0) == timestep[0]
    grow[...] = jnp.sum(jnp.where(here, gate[...], 0.0), axis=0, keepdims=True)
    complete(0)
    attend(0)
    share(1)
    share(2)
    relay(2)
    merge(0)
    text_core()
    complete(1)
    attend(1)
    text_attend()
    merge(1)
    complete(2)
    attend(2)
    merge(2)

    arrived(cr, r_c)
    for p in range(2):
        for h in range(NH):
            arrived(xr.at[p, h], r_x[p][h])
        arrived(sr.at[p], r_s[p])
    one, two = sr[0].reshape(NT, HD), sr[1].reshape(NT, HD)
    top = jnp.maximum(one, two)
    part1 = pltpu.roll(one, HD // 2, 1) * jnp.exp2((one - top) * SCALE2)
    part2 = pltpu.roll(two, HD // 2, 1) * jnp.exp2((two - top) * SCALE2)
    whole = part1 + part2
    shares = jnp.concatenate(
        [part1 / whole, part2 / whole, jnp.zeros((HD - 2 * NT, HD), jnp.float32)], axis=0
    ).T
    for src in range(NT):
        for h in range(NH):
            rows = slice(h * CHUNK, (h + 1) * CHUNK)
            joined = xr[0, h, src].astype(jnp.float32) * shares[rows, src : src + 1]
            joined += xr[1, h, src].astype(jnp.float32) * shares[rows, NT + src : NT + src + 1]
            joined += cr[src, :, h * HD : (h + 1) * HD].astype(jnp.float32)
            lo = (src * NH + h) * HD
            out_ref[:, lo : lo + HD] = joined.astype(jnp.bfloat16)

    for cp in sent:
        cp.wait_send()
    assert counts["s"] <= SENDS and counts["r"] <= RECVS, counts


def local(q_self, k_self, v_self, q_cross, k_text, v_text, text_len, timestep, gate_table):
    bf16, f32 = jnp.bfloat16, jnp.float32
    smem = pl.BlockSpec(memory_space=pltpu.SMEM)
    vmem = pl.BlockSpec(memory_space=pltpu.VMEM)
    hbm = pl.BlockSpec(memory_space=pltpu.HBM)
    return pl.pallas_call(
        kernel,
        out_shape=jax.ShapeDtypeStruct((CHUNK, NT * NH * HD), bf16),
        in_specs=[smem, smem, hbm, hbm, hbm, hbm, hbm, hbm, hbm],
        out_specs=vmem,
        scratch_shapes=[
            pltpu.VMEM((NH, NY, NX, ROWS, HD), bf16),
            pltpu.VMEM((NH, NY, NX, ROWS, HD), bf16),
            pltpu.VMEM((NH, 4, ROWS, HD), bf16),
            pltpu.VMEM((2, NH, ROWS // 2, HD), bf16),
            pltpu.VMEM((ROWS, NH * HD), bf16),
            pltpu.VMEM(gate_table.shape, f32),
            pltpu.VMEM((1, NH * HD), f32),
            pltpu.VMEM(k_text.shape, bf16),
            pltpu.VMEM(v_text.shape, bf16),
            pltpu.VMEM((4, 8, NH * HD), f32),
            pltpu.VMEM((8, NH * HD), f32),
            pltpu.VMEM((2, NY, NX, 16, NH * HD), bf16),
            pltpu.VMEM((NH, 4, HD, ROWS), f32),
            pltpu.VMEM((NH, 4, 2, ROWS), f32),
            pltpu.VMEM((NH, 2, HD, ROWS), f32),
            pltpu.VMEM((NH, 2, 2, ROWS), f32),
            pltpu.VMEM((2, NT, HD), f32),
            pltpu.VMEM((2, NH, NT, CHUNK, HD), bf16),
            pltpu.VMEM((2, NT, 1, HD), f32),
            pltpu.VMEM((2, NH, NT, CHUNK, HD), bf16),
            pltpu.VMEM((2, NT, 1, HD), f32),
            pltpu.VMEM((NT, CHUNK, NH * HD), bf16),
            pltpu.VMEM((NT, CHUNK, NH * HD), bf16),
            pltpu.SemaphoreType.DMA((SENDS,)),
            pltpu.SemaphoreType.DMA((RECVS,)),
            pltpu.SemaphoreType.DMA((16,)),
            pltpu.SemaphoreType.REGULAR,
            pltpu.SemaphoreType.REGULAR,
        ],
        compiler_params=pltpu.CompilerParams(
            collective_id=0, has_side_effects=True, vmem_limit_bytes=64 * 1024 * 1024
        ),
        name="gated_attention",
    )(text_len, timestep, q_self, k_self, v_self, q_cross, k_text, v_text, gate_table)


def solution(mesh):
    placed = (
        P("ctx", "tp"),
        P("ctx", "tp"),
        P("ctx", "tp"),
        P("ctx", "tp"),
        P("ctx", "tp"),
        P("ctx", "tp"),
        P(),
        P(),
        P(None, "tp"),
    )
    return jax.shard_map(
        local, mesh=mesh, in_specs=placed, out_specs=P(("ctx", "tp"), None), check_vma=False
    )
```

```python
import math

import jax
import jax.numpy as jnp
from jax import lax
from jax.experimental import pallas as pl
from jax.experimental.pallas import tpu as pltpu
from jax.sharding import PartitionSpec as P

HD = 128
ROWS = 128
NH = 3
NX = 4
NY = 4
NT = 8
CHUNK = ROWS // NT
KEYS = NX * NY * ROWS
TEXT = 2 * NX * NY * 16
SCALE2 = HD ** -0.5 * 1.4426950408889634
MESH_ID = pl.DeviceIdType.MESH
SENT = 8679
RECVS = 40


def kernel(
    text_len, timestep, q_ref, k_ref, v_ref, qc_ref, kt_ref, vt_ref, gate_ref, out_ref,
    kb, vb, qb, qf, qcb, gate, grow, ktv, vtv, txb, txf, tk, acc, racc, mst,
    xs, so, xr, sr, cs, cr, tally, ssem, rsem, lsem, near_sem, far_sem,
):
    ctx = lax.axis_index("ctx")
    zl = lax.axis_index("tp")
    y = ctx // 16
    zh = (ctx // 8) % 2
    x = (ctx // 2) % 4
    c = ctx % 2

    def dev(dy=0, dx=0, flip_c=False, dz=0):
        yy = (y + dy) % NY
        xx = (x + dx) % NX
        zz = (zh * NT + zl + dz + 2 * NT) % (2 * NT)
        cc = 1 - c if flip_c else c
        return (((yy * 2 + zz // NT) * 4 + xx) * 2 + cc, zz % NT)

    def owner(d, p):
        return (((y * 2 + (1 - zh if p else zh)) * 4 + x) * 2 + c, (zl + d) % NT)

    counts = {"bytes": 0, "r": 0, "l": 0}

    def new(kind):
        counts[kind] += 1
        return counts[kind] - 1

    def send(src, dst, rs, target):
        pltpu.make_async_remote_copy(
            src_ref=src, dst_ref=dst, send_sem=ssem.at[0], recv_sem=rsem.at[rs],
            device_id=target, device_id_type=MESH_ID,
        ).start()
        counts["bytes"] += math.prod(src.shape) * src.dtype.itemsize

    def arrived(ref, rs):
        pltpu.make_async_copy(ref, ref, rsem.at[rs]).wait()

    def fetch(src, dst, sem):
        cp = pltpu.make_async_copy(src, dst, lsem.at[sem])
        cp.start()
        return cp

    def signal(sem, target):
        pl.semaphore_signal(sem, inc=1, device_id=target, device_id_type=MESH_ID)

    def cols(h):
        return pl.ds(h * HD, HD)

    barrier = pltpu.get_barrier_semaphore()
    partners = [dev(dx=d) for d in (1, 2, 3)] + [dev(dy=d) for d in (1, 2, 3)]
    partners += [dev(flip_c=True)] + [dev(dz=d) for d in (1, -1, 2, -2)]
    for partner in partners:
        signal(barrier, partner)

    for h in range(NH):
        fetch(k_ref.at[:, cols(h)], kb.at[h, 0, 0], 0)
        fetch(v_ref.at[:, cols(h)], vb.at[h, 0, 0], 0)
        fetch(q_ref.at[:, cols(h)], qb.at[h, 3], 0)
    small = [fetch(kt_ref, ktv, 1), fetch(vt_ref, vtv, 2)]
    late = [fetch(qc_ref, qcb, 3), fetch(gate_ref, gate, 4)]
    pl.semaphore_wait(barrier, len(partners))

    sib = dev(flip_c=True)
    quarter = 4 - 8 * c

    def table(*shape):
        if not shape:
            return new("r")
        return [table(*shape[1:]) for unused in range(shape[0])]

    r_1, r_2, r_3 = table(NH), table(NH, 2), table(NH)
    r_qs, r_qf, r_qx, r_qy = table(), table(NH), table(NH), table()
    r_tf, r_tz, r_t, r_t3 = table(), table(), table(), table()
    r_acc, r_x, r_s, r_c = table(NH), table(), table(), table()
    plane = [(dy, dx) for dy in range(NY) for dx in range(NX) if dy + dx]

    def first(h):
        for d in (1, 3, 2):
            send(k_ref.at[:, cols(h)], kb.at[h, 0, 4 - d], r_1[h], dev(dx=d))
            send(v_ref.at[:, cols(h)], vb.at[h, 4 - d, 0], r_1[h], dev(dy=d))

    def halves(i):
        return pl.ds(2 * i, 2), pl.ds(2 - 2 * i, 2)

    def second(h):
        arrived(kb.at[h, pl.ds(0, 2), pl.ds(0, 3)], r_1[h])
        for step in range(2):
            for i, d in ((0, 1), (1, 3)):
                part = halves(i)[step]
                rs = r_3[h] if step else r_2[h][i]
                send(kb.at[h, 0, part], kb.at[h, 4 - d, part], rs, dev(dy=d))
                send(vb.at[h, part, 0], vb.at[h, part, 4 - d], rs, dev(dx=d))

    def relay(h):
        for i, d in ((0, 1), (1, 3)):
            part = halves(i)[0]
            arrived(kb.at[h, 0], r_2[h][i])
            send(kb.at[h, 4 - d, part], kb.at[h, 2, part], r_3[h], dev(dy=d))
            send(vb.at[h, part, 4 - d], vb.at[h, part, 2], r_3[h], dev(dx=d))

    def complete(h):
        arrived(kb.at[h], r_3[h])

    def cross(h):
        for i, d in ((0, 4), (1, -4)):
            rows = pl.ds(64 * i, 64)
            send(q_ref.at[rows, cols(h)], qf.at[i, h], r_qf[h], dev(dz=d))

    def pass_on(h):
        arrived(qb.at[h, 2], r_qf[h])
        for i, d in ((0, 4), (1, -4)):
            send(qf.at[i, h], qb.at[h, 2, pl.ds(64 * i, 64)], r_qx[h], dev(dz=d))

    def share(h):
        arrived(qb.at[h, 2], r_qx[h])
        send(qb.at[h, 2], qb.at[h, 0], r_qy, sib)

    def attend(h):
        scores = lax.dot_general(
            kb[h].reshape(KEYS, HD), qb[h].reshape(4 * ROWS, HD), (((1,), (1,)), ((), ())),
            preferred_element_type=jnp.float32,
        )
        top = jnp.max(scores, axis=0, keepdims=True)
        weights = jnp.exp2((scores - top) * SCALE2)
        total = jnp.sum(weights, axis=0, keepdims=True)
        product = lax.dot_general(
            vb[h].reshape(KEYS, HD), weights.astype(jnp.bfloat16), (((0,), (0,)), ((), ())),
            preferred_element_type=jnp.float32,
        )
        for b in range(4):
            lanes = slice(b * ROWS, (b + 1) * ROWS)
            acc[h, b, :HD] = product[:, lanes]
            acc[h, b, HD : HD + 1] = top[:, lanes]
            acc[h, b, HD + 1 : HD + 2] = total[:, lanes]
        send(acc.at[h, pl.ds(0, 2)], racc.at[h], r_acc[h], sib)

    def merge(h):
        arrived(racc.at[h], r_acc[h])
        for p in (1, 0):
            mine, yours = 3 - p, 1 - p
            one, two = acc[h, mine, HD : HD + 2], racc[h, yours, HD : HD + 2]
            top = jnp.maximum(one[:1], two[:1])
            f1 = jnp.exp2((one[:1] - top) * SCALE2)
            f2 = jnp.exp2((two[:1] - top) * SCALE2)
            total = one[1:] * f1 + two[1:] * f2
            mixed = acc[h, mine, :HD] * (f1 / total) + racc[h, yours, :HD] * (f2 / total)
            mixed = mixed.T * grow[:, h * HD : (h + 1) * HD]
            xs[p, h] = mixed.astype(jnp.bfloat16).reshape(NT, CHUNK, HD)
            lane = lax.broadcasted_iota(jnp.int32, (NT, HD), 1)
            packed = jnp.zeros((NT, HD), jnp.float32) if h == 0 else mst[p]
            for k, row in ((h, top), (4 + h, total)):
                moved = jnp.broadcast_to(row, (NT, HD))
                moved = pltpu.roll(moved, 0, 1, stride=CHUNK, stride_axis=0)
                moved = pltpu.roll(moved, (k + 1) * CHUNK % HD, 1)
                packed = jnp.where((lane >> 4) == k, moved, packed)
            if h < NH - 1:
                mst[p] = packed
            else:
                for i in range(NT):
                    so[p, NT - 1 - i] = packed[i : i + 1]
            for d in range(1 - p, NT):
                target = owner(d, p)
                to = (zl + d) % NT
                send(xs.at[p, h, to], xr.at[p, h, zl], r_x, target)
                if h == NH - 1:
                    send(so.at[p, to], sr.at[p, zl], r_s, target)
            if p == 0:
                pltpu.make_async_copy(xs.at[0, h, zl], xr.at[0, h, zl], rsem.at[r_x]).start()
                if h == NH - 1:
                    pltpu.make_async_copy(so.at[0, zl], sr.at[0, zl], rsem.at[r_s]).start()

    def text_tile():
        arrived(txf, r_tz)
        low, high = txb[0], txb[1]
        own = jnp.concatenate([low[:4], high[:4], low[4:], high[4:]], axis=0)
        tk[c, 0] = own.astype(jnp.bfloat16)
        for dy, dx in plane:
            slot = (-dy % NY) * NX + -dx % NX
            send(tk.at[c, 0], tk.at[c, slot], r_t, dev(dy=dy, dx=dx))

    def text_core():
        arrived(tk.at[c, pl.ds(1, NX * NY - 1)], r_t)
        send(tk.at[c], tk.at[c], r_t3, sib)

    def text_attend():
        arrived(tk.at[1 - c], r_t3)
        j = lax.broadcasted_iota(jnp.int32, (ROWS, TEXT), 1)
        jc, jy, jx = j >> 8, ((j >> 6) + y) & 3, ((j >> 4) + x) & 3
        jz, jr = (j >> 2) & 1, j & 3
        position = ((((jy * 2 + jz) * 4 + jx) * 2 + jc) << 2) + jr
        live = (position < text_len[0]) & ((j & 8) == 0)
        for h in range(NH):
            lanes = slice(h * HD, (h + 1) * HD)
            tiles = tk[:, :, :, lanes].reshape(TEXT, HD)
            scores = lax.dot_general(
                qcb[:, lanes], tiles, (((1,), (1,)), ((), ())), preferred_element_type=jnp.float32
            )
            scores = jnp.where(live, scores, -jnp.inf)
            top = jnp.max(scores, axis=1, keepdims=True)
            weights = jnp.exp2((scores - top) * SCALE2)
            total = jnp.sum(weights, axis=1, keepdims=True)
            moved = pltpu.roll(weights, 8, 1).astype(jnp.bfloat16)
            product = jnp.dot(moved, tiles, preferred_element_type=jnp.float32)
            cs[:, :, lanes] = (product / total).astype(jnp.bfloat16).reshape(NT, CHUNK, HD)
        for d in range(1, NT):
            send(cs.at[(zl + d) % NT], cr.at[zl], r_c, owner(d, 0))
        pltpu.make_async_copy(cs.at[zl], cr.at[zl], rsem.at[r_c]).start()

    for h in range(NH):
        first(h)
    for d in (2, -2):
        signal(near_sem, dev(dz=d))
    for h in range(NH):
        send(q_ref.at[:, cols(h)], qb.at[h, 1], r_qs, sib)
    for cp in small:
        cp.wait()
    txb[zh] = jnp.concatenate(
        [ktv[...].astype(jnp.float32), vtv[...].astype(jnp.float32)], axis=0
    )
    pl.semaphore_wait(near_sem, 2)
    for d in (4, -4):
        signal(far_sem, dev(dz=d))
    send(txb.at[zh], txf, r_tf, dev(dz=quarter))
    for h in range(NH):
        cross(h)
    nine = kb.at[:, 0, pl.ds(0, 3)]
    pltpu.make_async_copy(nine, nine, lsem.at[0]).wait()
    second(0)
    second(1)
    arrived(txf, r_tf)
    source = ((zh * NT + zl - quarter + 2 * NT) % (2 * NT)) // NT
    send(txf, txb.at[source], r_tz, dev(dz=quarter))
    pass_on(0)
    relay(0)
    second(2)
    pass_on(1)
    pass_on(2)
    for cp in late:
        cp.wait()
    here = lax.broadcasted_iota(jnp.int32, gate.shape, 0) == timestep[0]
    grow[...] = jnp.sum(jnp.where(here, gate[...], 0.0), axis=0, keepdims=True)
    text_tile()
    relay(1)
    pl.semaphore_wait(far_sem, 2)
    share(0)
    share(1)
    text_core()
    relay(2)
    share(2)
    text_attend()
    three = kb.at[0, 0, pl.ds(0, 3)]
    arrived(three, r_qs)
    arrived(three, r_qy)
    complete(0)
    attend(0)
    merge(0)
    complete(1)
    attend(1)
    complete(2)
    attend(2)
    merge(1)
    merge(2)

    arrived(cr, r_c)
    arrived(xr, r_x)
    arrived(sr, r_s)
    one, two = sr[0].reshape(NT, HD), sr[1].reshape(NT, HD)
    top = jnp.maximum(one, two)
    part1 = pltpu.roll(one, HD // 2, 1) * jnp.exp2((one - top) * SCALE2)
    part2 = pltpu.roll(two, HD // 2, 1) * jnp.exp2((two - top) * SCALE2)
    whole = part1 + part2
    shares = jnp.concatenate(
        [part1 / whole, part2 / whole, jnp.zeros((HD - 2 * NT, HD), jnp.float32)], axis=0
    ).T
    for src in range(NT):
        for h in range(NH):
            rows = slice(h * CHUNK, (h + 1) * CHUNK)
            joined = xr[0, h, src].astype(jnp.float32) * shares[rows, src : src + 1]
            joined += xr[1, h, src].astype(jnp.float32) * shares[rows, NT + src : NT + src + 1]
            joined += cr[src, :, h * HD : (h + 1) * HD].astype(jnp.float32)
            lo = (src * NH + h) * HD
            out_ref[:, lo : lo + HD] = joined.astype(jnp.bfloat16)

    assert counts["bytes"] == SENT * 512 and counts["r"] <= RECVS, counts
    pltpu.make_async_copy(tally, tally, ssem.at[0]).wait()


def local(q_self, k_self, v_self, q_cross, k_text, v_text, text_len, timestep, gate_table):
    bf16, f32 = jnp.bfloat16, jnp.float32
    smem = pl.BlockSpec(memory_space=pltpu.SMEM)
    vmem = pl.BlockSpec(memory_space=pltpu.VMEM)
    hbm = pl.BlockSpec(memory_space=pltpu.HBM)
    return pl.pallas_call(
        kernel,
        out_shape=jax.ShapeDtypeStruct((CHUNK, NT * NH * HD), bf16),
        in_specs=[smem, smem, hbm, hbm, hbm, hbm, hbm, hbm, hbm],
        out_specs=vmem,
        scratch_shapes=[
            pltpu.VMEM((NH, NY, NX, ROWS, HD), bf16),
            pltpu.VMEM((NH, NY, NX, ROWS, HD), bf16),
            pltpu.VMEM((NH, 4, ROWS, HD), bf16),
            pltpu.VMEM((2, NH, ROWS // 2, HD), bf16),
            pltpu.VMEM((ROWS, NH * HD), bf16),
            pltpu.VMEM(gate_table.shape, f32),
            pltpu.VMEM((1, NH * HD), f32),
            pltpu.VMEM(k_text.shape, bf16),
            pltpu.VMEM(v_text.shape, bf16),
            pltpu.VMEM((2, 8, NH * HD), f32),
            pltpu.VMEM((8, NH * HD), f32),
            pltpu.VMEM((2, NY * NX, 16, NH * HD), bf16),
            pltpu.VMEM((NH, 4, HD + 8, ROWS), f32),
            pltpu.VMEM((NH, 2, HD + 8, ROWS), f32),
            pltpu.VMEM((2, NT, HD), f32),
            pltpu.VMEM((2, NH, NT, CHUNK, HD), bf16),
            pltpu.VMEM((2, NT, 1, HD), f32),
            pltpu.VMEM((2, NH, NT, CHUNK, HD), bf16),
            pltpu.VMEM((2, NT, 1, HD), f32),
            pltpu.VMEM((NT, CHUNK, NH * HD), bf16),
            pltpu.VMEM((NT, CHUNK, NH * HD), bf16),
            pltpu.VMEM((SENT, HD), f32),
            pltpu.SemaphoreType.DMA((1,)),
            pltpu.SemaphoreType.DMA((RECVS,)),
            pltpu.SemaphoreType.DMA((5,)),
            pltpu.SemaphoreType.REGULAR,
            pltpu.SemaphoreType.REGULAR,
        ],
        compiler_params=pltpu.CompilerParams(
            collective_id=0, has_side_effects=True, vmem_limit_bytes=64 * 1024 * 1024
        ),
        name="gated_attention",
    )(text_len, timestep, q_self, k_self, v_self, q_cross, k_text, v_text, gate_table)


def solution(mesh):
    placed = (
        P("ctx", "tp"),
        P("ctx", "tp"),
        P("ctx", "tp"),
        P("ctx", "tp"),
        P("ctx", "tp"),
        P("ctx", "tp"),
        P(),
        P(),
        P(None, "tp"),
    )
    return jax.shard_map(
        local, mesh=mesh, in_specs=placed, out_specs=P(("ctx", "tp"), None), check_vma=False
    )
```

```python
import math

import jax
import jax.numpy as jnp
from jax import lax
from jax.experimental import pallas as pl
from jax.experimental.pallas import tpu as pltpu
from jax.sharding import PartitionSpec as P

HD = 128
ROWS = 128
NH = 3
NX = 4
NY = 4
NT = 8
CHUNK = ROWS // NT
KEYS = NX * NY * ROWS
TEXT = 2 * NX * NY * 16
SCALE2 = HD ** -0.5 * 1.4426950408889634
MESH_ID = pl.DeviceIdType.MESH
SENT = 8679
RECVS = 40


def kernel(
    text_len, timestep, q_ref, k_ref, v_ref, qc_ref, kt_ref, vt_ref, gate_ref, out_ref,
    kb, vb, qb, qf, qcb, gate, grow, ktv, vtv, txb, txf, tk, acc, racc, mst,
    xs, so, xr, sr, cs, cr, tally, ssem, rsem, lsem, near_sem, far_sem,
):
    ctx = lax.axis_index("ctx")
    zl = lax.axis_index("tp")
    y = ctx // 16
    zh = (ctx // 8) % 2
    x = (ctx // 2) % 4
    c = ctx % 2

    def dev(dy=0, dx=0, flip_c=False, dz=0):
        yy = (y + dy) % NY
        xx = (x + dx) % NX
        zz = (zh * NT + zl + dz + 2 * NT) % (2 * NT)
        cc = 1 - c if flip_c else c
        return (((yy * 2 + zz // NT) * 4 + xx) * 2 + cc, zz % NT)

    def owner(d, p):
        return (((y * 2 + (1 - zh if p else zh)) * 4 + x) * 2 + c, (zl + d) % NT)

    counts = {"bytes": 0, "r": 0, "l": 0}

    def new(kind):
        counts[kind] += 1
        return counts[kind] - 1

    def send(src, dst, rs, target):
        pltpu.make_async_remote_copy(
            src_ref=src, dst_ref=dst, send_sem=ssem.at[0], recv_sem=rsem.at[rs],
            device_id=target, device_id_type=MESH_ID,
        ).start()
        counts["bytes"] += math.prod(src.shape) * src.dtype.itemsize

    def arrived(ref, rs):
        pltpu.make_async_copy(ref, ref, rsem.at[rs]).wait()

    def fetch(src, dst, sem):
        cp = pltpu.make_async_copy(src, dst, lsem.at[sem])
        cp.start()
        return cp

    def signal(sem, target):
        pl.semaphore_signal(sem, inc=1, device_id=target, device_id_type=MESH_ID)

    def cols(h):
        return pl.ds(h * HD, HD)

    barrier = pltpu.get_barrier_semaphore()
    partners = [dev(dx=d) for d in (1, 2, 3)] + [dev(dy=d) for d in (1, 2, 3)]
    partners += [dev(flip_c=True)] + [dev(dz=d) for d in (1, -1, 2, -2)]
    for partner in partners:
        signal(barrier, partner)

    for h in range(NH):
        fetch(k_ref.at[:, cols(h)], kb.at[h, 0, 0], 0)
        fetch(v_ref.at[:, cols(h)], vb.at[h, 0, 0], 0)
        fetch(q_ref.at[:, cols(h)], qb.at[h, 3], 0)
    small = [fetch(kt_ref, ktv, 1), fetch(vt_ref, vtv, 2)]
    late = [fetch(qc_ref, qcb, 3), fetch(gate_ref, gate, 4)]
    pl.semaphore_wait(barrier, len(partners))

    sib = dev(flip_c=True)
    quarter = 4 - 8 * c

    def table(*shape):
        if not shape:
            return new("r")
        return [table(*shape[1:]) for unused in range(shape[0])]

    r_1, r_2, r_3 = table(NH), table(NH, 2), table(NH)
    r_qs, r_qf, r_qx, r_qy = table(), table(NH), table(NH), table()
    r_tf, r_tz, r_t, r_t3 = table(), table(), table(), table()
    r_acc, r_x, r_s, r_c = table(NH), table(), table(), table()
    plane = [(dy, dx) for dy in range(NY) for dx in range(NX) if dy + dx]

    def first(h):
        for d in (1, 3, 2):
            send(k_ref.at[:, cols(h)], kb.at[h, 0, 4 - d], r_1[h], dev(dx=d))
            send(v_ref.at[:, cols(h)], vb.at[h, 4 - d, 0], r_1[h], dev(dy=d))

    def halves(i):
        return pl.ds(2 * i, 2), pl.ds(2 - 2 * i, 2)

    def second(h):
        arrived(kb.at[h, pl.ds(0, 2), pl.ds(0, 3)], r_1[h])
        for step in range(2):
            for i, d in ((0, 1), (1, 3)):
                part = halves(i)[step]
                rs = r_3[h] if step else r_2[h][i]
                send(kb.at[h, 0, part], kb.at[h, 4 - d, part], rs, dev(dy=d))
                send(vb.at[h, part, 0], vb.at[h, part, 4 - d], rs, dev(dx=d))

    def relay(h):
        for i, d in ((0, 1), (1, 3)):
            part = halves(i)[0]
            arrived(kb.at[h, 0], r_2[h][i])
            send(kb.at[h, 4 - d, part], kb.at[h, 2, part], r_3[h], dev(dy=d))
            send(vb.at[h, part, 4 - d], vb.at[h, part, 2], r_3[h], dev(dx=d))

    def complete(h):
        arrived(kb.at[h], r_3[h])

    def cross(h):
        for i, d in ((0, 4), (1, -4)):
            rows = pl.ds(64 * i, 64)
            send(q_ref.at[rows, cols(h)], qf.at[i, h], r_qf[h], dev(dz=d))

    def pass_on(h):
        arrived(qb.at[h, 2], r_qf[h])
        for i, d in ((0, 4), (1, -4)):
            send(qf.at[i, h], qb.at[h, 2, pl.ds(64 * i, 64)], r_qx[h], dev(dz=d))

    def share(h):
        arrived(qb.at[h, 2], r_qx[h])
        send(qb.at[h, 2], qb.at[h, 0], r_qy, sib)

    def attend(h):
        scores = lax.dot_general(
            kb[h].reshape(KEYS, HD), qb[h].reshape(4 * ROWS, HD), (((1,), (1,)), ((), ())),
            preferred_element_type=jnp.float32,
        )
        top = jnp.max(scores, axis=0, keepdims=True)
        weights = jnp.exp2((scores - top) * SCALE2)
        total = jnp.sum(weights, axis=0, keepdims=True)
        product = lax.dot_general(
            vb[h].reshape(KEYS, HD), weights.astype(jnp.bfloat16), (((0,), (0,)), ((), ())),
            preferred_element_type=jnp.float32,
        )
        for b in range(4):
            lanes = slice(b * ROWS, (b + 1) * ROWS)
            acc[h, b, :HD] = product[:, lanes]
            acc[h, b, HD : HD + 1] = top[:, lanes]
            acc[h, b, HD + 1 : HD + 2] = total[:, lanes]
        send(acc.at[h, pl.ds(0, 2)], racc.at[h], r_acc[h], sib)

    def merge(h):
        arrived(racc.at[h], r_acc[h])
        for p in (1, 0):
            mine, yours = 3 - p, 1 - p
            one, two = acc[h, mine, HD : HD + 2], racc[h, yours, HD : HD + 2]
            top = jnp.maximum(one[:1], two[:1])
            f1 = jnp.exp2((one[:1] - top) * SCALE2)
            f2 = jnp.exp2((two[:1] - top) * SCALE2)
            total = one[1:] * f1 + two[1:] * f2
            mixed = acc[h, mine, :HD] * (f1 / total) + racc[h, yours, :HD] * (f2 / total)
            mixed = mixed.T * grow[:, h * HD : (h + 1) * HD]
            xs[p, h] = mixed.astype(jnp.bfloat16).reshape(NT, CHUNK, HD)
            lane = lax.broadcasted_iota(jnp.int32, (NT, HD), 1)
            packed = jnp.zeros((NT, HD), jnp.float32) if h == 0 else mst[p]
            for k, row in ((h, top), (4 + h, total)):
                moved = jnp.broadcast_to(row, (NT, HD))
                moved = pltpu.roll(moved, 0, 1, stride=CHUNK, stride_axis=0)
                moved = pltpu.roll(moved, (k + 1) * CHUNK % HD, 1)
                packed = jnp.where((lane >> 4) == k, moved, packed)
            if h < NH - 1:
                mst[p] = packed
            else:
                for i in range(NT):
                    so[p, NT - 1 - i] = packed[i : i + 1]
            for d in range(1 - p, NT):
                target = owner(d, p)
                to = (zl + d) % NT
                send(xs.at[p, h, to], xr.at[p, h, zl], r_x, target)
                if h == NH - 1:
                    send(so.at[p, to], sr.at[p, zl], r_s, target)
            if p == 0:
                pltpu.make_async_copy(xs.at[0, h, zl], xr.at[0, h, zl], rsem.at[r_x]).start()
                if h == NH - 1:
                    pltpu.make_async_copy(so.at[0, zl], sr.at[0, zl], rsem.at[r_s]).start()

    def text_tile():
        arrived(txf, r_tz)
        low, high = txb[0], txb[1]
        own = jnp.concatenate([low[:4], high[:4], low[4:], high[4:]], axis=0)
        tk[c, 0] = own.astype(jnp.bfloat16)
        for dy, dx in plane:
            slot = (-dy % NY) * NX + -dx % NX
            send(tk.at[c, 0], tk.at[c, slot], r_t, dev(dy=dy, dx=dx))

    def text_core():
        arrived(tk.at[c, pl.ds(1, NX * NY - 1)], r_t)
        send(tk.at[c], tk.at[c], r_t3, sib)

    def text_attend():
        arrived(tk.at[1 - c], r_t3)
        j = lax.broadcasted_iota(jnp.int32, (ROWS, TEXT), 1)
        jc, jy, jx = j >> 8, ((j >> 6) + y) & 3, ((j >> 4) + x) & 3
        jz, jr = (j >> 2) & 1, j & 3
        position = ((((jy * 2 + jz) * 4 + jx) * 2 + jc) << 2) + jr
        live = (position < text_len[0]) & ((j & 8) == 0)
        for h in range(NH):
            lanes = slice(h * HD, (h + 1) * HD)
            tiles = tk[:, :, :, lanes].reshape(TEXT, HD)
            scores = lax.dot_general(
                qcb[:, lanes], tiles, (((1,), (1,)), ((), ())), preferred_element_type=jnp.float32
            )
            scores = jnp.where(live, scores, -jnp.inf)
            top = jnp.max(scores, axis=1, keepdims=True)
            weights = jnp.exp2((scores - top) * SCALE2)
            total = jnp.sum(weights, axis=1, keepdims=True)
            moved = pltpu.roll(weights, 8, 1).astype(jnp.bfloat16)
            product = jnp.dot(moved, tiles, preferred_element_type=jnp.float32)
            cs[:, :, lanes] = (product / total).astype(jnp.bfloat16).reshape(NT, CHUNK, HD)
        for d in range(1, NT):
            send(cs.at[(zl + d) % NT], cr.at[zl], r_c, owner(d, 0))
        pltpu.make_async_copy(cs.at[zl], cr.at[zl], rsem.at[r_c]).start()

    for h in range(NH):
        first(h)
    for d in (2, -2):
        signal(near_sem, dev(dz=d))
    for h in range(NH):
        send(q_ref.at[:, cols(h)], qb.at[h, 1], r_qs, sib)
    for cp in small:
        cp.wait()
    txb[zh] = jnp.concatenate(
        [ktv[...].astype(jnp.float32), vtv[...].astype(jnp.float32)], axis=0
    )
    pl.semaphore_wait(near_sem, 2)
    for d in (4, -4):
        signal(far_sem, dev(dz=d))
    send(txb.at[zh], txf, r_tf, dev(dz=quarter))
    for h in range(NH):
        cross(h)
    nine = kb.at[:, 0, pl.ds(0, 3)]
    pltpu.make_async_copy(nine, nine, lsem.at[0]).wait()
    second(0)
    second(1)
    arrived(txf, r_tf)
    source = ((zh * NT + zl - quarter + 2 * NT) % (2 * NT)) // NT
    send(txf, txb.at[source], r_tz, dev(dz=quarter))
    pass_on(0)
    relay(0)
    pass_on(1)
    text_tile()
    second(2)
    pass_on(2)
    for cp in late:
        cp.wait()
    here = lax.broadcasted_iota(jnp.int32, gate.shape, 0) == timestep[0]
    grow[...] = jnp.sum(jnp.where(here, gate[...], 0.0), axis=0, keepdims=True)
    relay(1)
    pl.semaphore_wait(far_sem, 2)
    share(0)
    share(1)
    text_core()
    relay(2)
    share(2)
    text_attend()
    three = kb.at[0, 0, pl.ds(0, 3)]
    arrived(three, r_qs)
    arrived(three, r_qy)
    complete(0)
    attend(0)
    merge(0)
    complete(1)
    attend(1)
    complete(2)
    attend(2)
    merge(1)
    merge(2)

    arrived(cr, r_c)
    arrived(xr, r_x)
    arrived(sr, r_s)
    one, two = sr[0].reshape(NT, HD), sr[1].reshape(NT, HD)
    top = jnp.maximum(one, two)
    part1 = pltpu.roll(one, HD // 2, 1) * jnp.exp2((one - top) * SCALE2)
    part2 = pltpu.roll(two, HD // 2, 1) * jnp.exp2((two - top) * SCALE2)
    whole = part1 + part2
    shares = jnp.concatenate(
        [part1 / whole, part2 / whole, jnp.zeros((HD - 2 * NT, HD), jnp.float32)], axis=0
    ).T
    for src in range(NT):
        for h in range(NH):
            rows = slice(h * CHUNK, (h + 1) * CHUNK)
            joined = xr[0, h, src].astype(jnp.float32) * shares[rows, src : src + 1]
            joined += xr[1, h, src].astype(jnp.float32) * shares[rows, NT + src : NT + src + 1]
            joined += cr[src, :, h * HD : (h + 1) * HD].astype(jnp.float32)
            lo = (src * NH + h) * HD
            out_ref[:, lo : lo + HD] = joined.astype(jnp.bfloat16)

    assert counts["bytes"] == SENT * 512 and counts["r"] <= RECVS, counts
    pltpu.make_async_copy(tally, tally, ssem.at[0]).wait()


def local(q_self, k_self, v_self, q_cross, k_text, v_text, text_len, timestep, gate_table):
    bf16, f32 = jnp.bfloat16, jnp.float32
    smem = pl.BlockSpec(memory_space=pltpu.SMEM)
    vmem = pl.BlockSpec(memory_space=pltpu.VMEM)
    hbm = pl.BlockSpec(memory_space=pltpu.HBM)
    return pl.pallas_call(
        kernel,
        out_shape=jax.ShapeDtypeStruct((CHUNK, NT * NH * HD), bf16),
        in_specs=[smem, smem, hbm, hbm, hbm, hbm, hbm, hbm, hbm],
        out_specs=vmem,
        scratch_shapes=[
            pltpu.VMEM((NH, NY, NX, ROWS, HD), bf16),
            pltpu.VMEM((NH, NY, NX, ROWS, HD), bf16),
            pltpu.VMEM((NH, 4, ROWS, HD), bf16),
            pltpu.VMEM((2, NH, ROWS // 2, HD), bf16),
            pltpu.VMEM((ROWS, NH * HD), bf16),
            pltpu.VMEM(gate_table.shape, f32),
            pltpu.VMEM((1, NH * HD), f32),
            pltpu.VMEM(k_text.shape, bf16),
            pltpu.VMEM(v_text.shape, bf16),
            pltpu.VMEM((2, 8, NH * HD), f32),
            pltpu.VMEM((8, NH * HD), f32),
            pltpu.VMEM((2, NY * NX, 16, NH * HD), bf16),
            pltpu.VMEM((NH, 4, HD + 8, ROWS), f32),
            pltpu.VMEM((NH, 2, HD + 8, ROWS), f32),
            pltpu.VMEM((2, NT, HD), f32),
            pltpu.VMEM((2, NH, NT, CHUNK, HD), bf16),
            pltpu.VMEM((2, NT, 1, HD), f32),
            pltpu.VMEM((2, NH, NT, CHUNK, HD), bf16),
            pltpu.VMEM((2, NT, 1, HD), f32),
            pltpu.VMEM((NT, CHUNK, NH * HD), bf16),
            pltpu.VMEM((NT, CHUNK, NH * HD), bf16),
            pltpu.VMEM((SENT, HD), f32),
            pltpu.SemaphoreType.DMA((1,)),
            pltpu.SemaphoreType.DMA((RECVS,)),
            pltpu.SemaphoreType.DMA((5,)),
            pltpu.SemaphoreType.REGULAR,
            pltpu.SemaphoreType.REGULAR,
        ],
        compiler_params=pltpu.CompilerParams(
            collective_id=0, has_side_effects=True, vmem_limit_bytes=64 * 1024 * 1024
        ),
        name="gated_attention",
    )(text_len, timestep, q_self, k_self, v_self, q_cross, k_text, v_text, gate_table)


def solution(mesh):
    placed = (
        P("ctx", "tp"),
        P("ctx", "tp"),
        P("ctx", "tp"),
        P("ctx", "tp"),
        P("ctx", "tp"),
        P("ctx", "tp"),
        P(),
        P(),
        P(None, "tp"),
    )
    return jax.shard_map(
        local, mesh=mesh, in_specs=placed, out_specs=P(("ctx", "tp"), None), check_vma=False
    )
```

```python
import math

import jax
import jax.numpy as jnp
from jax import lax
from jax.experimental import pallas as pl
from jax.experimental.pallas import tpu as pltpu
from jax.sharding import PartitionSpec as P

HD = 128
ROWS = 128
NH = 3
NX = 4
NY = 4
NT = 8
CHUNK = ROWS // NT
KEYS = NX * NY * ROWS
TEXT = 2 * NX * NY * 16
SCALE2 = HD ** -0.5 * 1.4426950408889634
MESH_ID = pl.DeviceIdType.MESH
SENT = 8679
RECVS = 40


def kernel(
    text_len, timestep, q_ref, k_ref, v_ref, qc_ref, kt_ref, vt_ref, gate_ref, out_ref,
    kb, vb, qb, qf, qcb, gate, grow, ktv, vtv, txb, txf, tk, acc, racc, mst,
    xs, so, xr, sr, cs, cr, tally, ssem, rsem, lsem, near_sem, far_sem,
):
    ctx = lax.axis_index("ctx")
    zl = lax.axis_index("tp")
    y = ctx // 16
    zh = (ctx // 8) % 2
    x = (ctx // 2) % 4
    c = ctx % 2

    def dev(dy=0, dx=0, flip_c=False, dz=0):
        yy = (y + dy) % NY
        xx = (x + dx) % NX
        zz = (zh * NT + zl + dz + 2 * NT) % (2 * NT)
        cc = 1 - c if flip_c else c
        return (((yy * 2 + zz // NT) * 4 + xx) * 2 + cc, zz % NT)

    def owner(d, p):
        return (((y * 2 + (1 - zh if p else zh)) * 4 + x) * 2 + c, (zl + d) % NT)

    counts = {"bytes": 0, "r": 0, "l": 0}

    def new(kind):
        counts[kind] += 1
        return counts[kind] - 1

    def send(src, dst, rs, target):
        pltpu.make_async_remote_copy(
            src_ref=src, dst_ref=dst, send_sem=ssem.at[0], recv_sem=rsem.at[rs],
            device_id=target, device_id_type=MESH_ID,
        ).start()
        counts["bytes"] += math.prod(src.shape) * src.dtype.itemsize

    def arrived(ref, rs):
        pltpu.make_async_copy(ref, ref, rsem.at[rs]).wait()

    def fetch(src, dst, sem):
        cp = pltpu.make_async_copy(src, dst, lsem.at[sem])
        cp.start()
        return cp

    def signal(sem, target):
        pl.semaphore_signal(sem, inc=1, device_id=target, device_id_type=MESH_ID)

    def cols(h):
        return pl.ds(h * HD, HD)

    barrier = pltpu.get_barrier_semaphore()
    partners = [dev(dx=d) for d in (1, 2, 3)] + [dev(dy=d) for d in (1, 2, 3)]
    partners += [dev(flip_c=True)] + [dev(dz=d) for d in (1, -1, 2, -2)]
    for partner in partners:
        signal(barrier, partner)

    for h in range(NH):
        fetch(k_ref.at[:, cols(h)], kb.at[h, 0, 0], 0)
        fetch(v_ref.at[:, cols(h)], vb.at[h, 0, 0], 0)
        fetch(q_ref.at[:, cols(h)], qb.at[h, 3], 0)
    small = [fetch(kt_ref, ktv, 1), fetch(vt_ref, vtv, 2)]
    late = [fetch(qc_ref, qcb, 3), fetch(gate_ref, gate, 4)]
    pl.semaphore_wait(barrier, len(partners))

    sib = dev(flip_c=True)
    quarter = 4 - 8 * c

    def table(*shape):
        if not shape:
            return new("r")
        return [table(*shape[1:]) for unused in range(shape[0])]

    r_1, r_2, r_3 = table(NH), table(NH, 2), table(NH)
    r_qs, r_qf, r_qx, r_qy = table(), table(NH), table(NH), table()
    r_tf, r_tz, r_t, r_t3 = table(), table(), table(), table()
    r_acc, r_x, r_s, r_c = table(NH), table(), table(), table()
    plane = [(dy, dx) for dy in range(NY) for dx in range(NX) if dy + dx]

    def first(h):
        for d in (1, 3, 2):
            send(k_ref.at[:, cols(h)], kb.at[h, 0, 4 - d], r_1[h], dev(dx=d))
            send(v_ref.at[:, cols(h)], vb.at[h, 4 - d, 0], r_1[h], dev(dy=d))

    def halves(i):
        return pl.ds(2 * i, 2), pl.ds(2 - 2 * i, 2)

    def second(h):
        arrived(kb.at[h, pl.ds(0, 2), pl.ds(0, 3)], r_1[h])
        for step in range(2):
            for i, d in ((0, 1), (1, 3)):
                part = halves(i)[step]
                rs = r_3[h] if step else r_2[h][i]
                send(kb.at[h, 0, part], kb.at[h, 4 - d, part], rs, dev(dy=d))
                send(vb.at[h, part, 0], vb.at[h, part, 4 - d], rs, dev(dx=d))

    def relay(h):
        for i, d in ((0, 1), (1, 3)):
            part = halves(i)[0]
            arrived(kb.at[h, 0], r_2[h][i])
            send(kb.at[h, 4 - d, part], kb.at[h, 2, part], r_3[h], dev(dy=d))
            send(vb.at[h, part, 4 - d], vb.at[h, part, 2], r_3[h], dev(dx=d))

    def complete(h):
        arrived(kb.at[h], r_3[h])

    def cross(h):
        for i, d in ((0, 4), (1, -4)):
            rows = pl.ds(64 * i, 64)
            send(q_ref.at[rows, cols(h)], qf.at[i, h], r_qf[h], dev(dz=d))

    def pass_on(h):
        arrived(qb.at[h, 2], r_qf[h])
        for i, d in ((0, 4), (1, -4)):
            send(qf.at[i, h], qb.at[h, 2, pl.ds(64 * i, 64)], r_qx[h], dev(dz=d))

    def share(h):
        arrived(qb.at[h, 2], r_qx[h])
        send(qb.at[h, 2], qb.at[h, 0], r_qy, sib)

    def attend(h):
        scores = lax.dot_general(
            kb[h].reshape(KEYS, HD), qb[h].reshape(4 * ROWS, HD), (((1,), (1,)), ((), ())),
            preferred_element_type=jnp.float32,
        )
        top = jnp.max(scores, axis=0, keepdims=True)
        weights = jnp.exp2((scores - top) * SCALE2)
        total = jnp.sum(weights, axis=0, keepdims=True)
        product = lax.dot_general(
            vb[h].reshape(KEYS, HD), weights.astype(jnp.bfloat16), (((0,), (0,)), ((), ())),
            preferred_element_type=jnp.float32,
        )
        for b in range(4):
            lanes = slice(b * ROWS, (b + 1) * ROWS)
            acc[h, b, :HD] = product[:, lanes]
            acc[h, b, HD : HD + 1] = top[:, lanes]
            acc[h, b, HD + 1 : HD + 2] = total[:, lanes]
        send(acc.at[h, pl.ds(0, 2)], racc.at[h], r_acc[h], sib)

    def merge(h):
        arrived(racc.at[h], r_acc[h])
        for p in (1, 0):
            mine, yours = 3 - p, 1 - p
            one, two = acc[h, mine, HD : HD + 2], racc[h, yours, HD : HD + 2]
            top = jnp.maximum(one[:1], two[:1])
            f1 = jnp.exp2((one[:1] - top) * SCALE2)
            f2 = jnp.exp2((two[:1] - top) * SCALE2)
            total = one[1:] * f1 + two[1:] * f2
            mixed = acc[h, mine, :HD] * (f1 / total) + racc[h, yours, :HD] * (f2 / total)
            mixed = mixed.T * grow[:, h * HD : (h + 1) * HD]
            xs[p, h] = mixed.astype(jnp.bfloat16).reshape(NT, CHUNK, HD)
            lane = lax.broadcasted_iota(jnp.int32, (NT, HD), 1)
            packed = jnp.zeros((NT, HD), jnp.float32) if h == 0 else mst[p]
            for k, row in ((h, top), (4 + h, total)):
                moved = jnp.broadcast_to(row, (NT, HD))
                moved = pltpu.roll(moved, 0, 1, stride=CHUNK, stride_axis=0)
                moved = pltpu.roll(moved, (k + 1) * CHUNK % HD, 1)
                packed = jnp.where((lane >> 4) == k, moved, packed)
            if h < NH - 1:
                mst[p] = packed
            else:
                for i in range(NT):
                    so[p, NT - 1 - i] = packed[i : i + 1]
            for d in range(1 - p, NT):
                target = owner(d, p)
                to = (zl + d) % NT
                send(xs.at[p, h, to], xr.at[p, h, zl], r_x, target)
                if h == NH - 1:
                    send(so.at[p, to], sr.at[p, zl], r_s, target)
            if p == 0:
                pltpu.make_async_copy(xs.at[0, h, zl], xr.at[0, h, zl], rsem.at[r_x]).start()
                if h == NH - 1:
                    pltpu.make_async_copy(so.at[0, zl], sr.at[0, zl], rsem.at[r_s]).start()

    def text_tile():
        arrived(txf, r_tz)
        low, high = txb[0], txb[1]
        own = jnp.concatenate([low[:4], high[:4], low[4:], high[4:]], axis=0)
        tk[c, 0] = own.astype(jnp.bfloat16)
        for dy, dx in plane:
            slot = (-dy % NY) * NX + -dx % NX
            send(tk.at[c, 0], tk.at[c, slot], r_t, dev(dy=dy, dx=dx))

    def text_core():
        arrived(tk.at[c, pl.ds(1, NX * NY - 1)], r_t)
        send(tk.at[c], tk.at[c], r_t3, sib)

    def text_attend():
        arrived(tk.at[1 - c], r_t3)
        j = lax.broadcasted_iota(jnp.int32, (ROWS, TEXT), 1)
        jc, jy, jx = j >> 8, ((j >> 6) + y) & 3, ((j >> 4) + x) & 3
        jz, jr = (j >> 2) & 1, j & 3
        position = ((((jy * 2 + jz) * 4 + jx) * 2 + jc) << 2) + jr
        live = (position < text_len[0]) & ((j & 8) == 0)
        for h in range(NH):
            lanes = slice(h * HD, (h + 1) * HD)
            tiles = tk[:, :, :, lanes].reshape(TEXT, HD)
            scores = lax.dot_general(
                qcb[:, lanes], tiles, (((1,), (1,)), ((), ())), preferred_element_type=jnp.float32
            )
            scores = jnp.where(live, scores, -jnp.inf)
            top = jnp.max(scores, axis=1, keepdims=True)
            weights = jnp.exp2((scores - top) * SCALE2)
            total = jnp.sum(weights, axis=1, keepdims=True)
            moved = pltpu.roll(weights, 8, 1).astype(jnp.bfloat16)
            product = jnp.dot(moved, tiles, preferred_element_type=jnp.float32)
            cs[:, :, lanes] = (product / total).astype(jnp.bfloat16).reshape(NT, CHUNK, HD)
        for d in range(1, NT):
            send(cs.at[(zl + d) % NT], cr.at[zl], r_c, owner(d, 0))
        pltpu.make_async_copy(cs.at[zl], cr.at[zl], rsem.at[r_c]).start()

    for h in range(NH):
        first(h)
    for d in (2, -2):
        signal(near_sem, dev(dz=d))
    for h in range(NH):
        send(q_ref.at[:, cols(h)], qb.at[h, 1], r_qs, sib)
    for cp in small:
        cp.wait()
    txb[zh] = jnp.concatenate(
        [ktv[...].astype(jnp.float32), vtv[...].astype(jnp.float32)], axis=0
    )
    pl.semaphore_wait(near_sem, 2)
    for d in (4, -4):
        signal(far_sem, dev(dz=d))
    send(txb.at[zh], txf, r_tf, dev(dz=quarter))
    for h in range(NH):
        cross(h)
    nine = kb.at[:, 0, pl.ds(0, 3)]
    pltpu.make_async_copy(nine, nine, lsem.at[0]).wait()
    second(0)
    second(1)
    arrived(txf, r_tf)
    source = ((zh * NT + zl - quarter + 2 * NT) % (2 * NT)) // NT
    send(txf, txb.at[source], r_tz, dev(dz=quarter))
    pass_on(0)
    relay(0)
    pass_on(1)
    text_tile()
    second(2)
    pass_on(2)
    for cp in late:
        cp.wait()
    here = lax.broadcasted_iota(jnp.int32, gate.shape, 0) == timestep[0]
    grow[...] = jnp.sum(jnp.where(here, gate[...], 0.0), axis=0, keepdims=True)
    relay(1)
    pl.semaphore_wait(far_sem, 2)
    share(0)
    text_core()
    share(1)
    relay(2)
    share(2)
    text_attend()
    three = kb.at[0, 0, pl.ds(0, 3)]
    arrived(three, r_qs)
    arrived(three, r_qy)
    complete(0)
    attend(0)
    merge(0)
    complete(1)
    attend(1)
    complete(2)
    attend(2)
    merge(1)
    merge(2)

    arrived(cr, r_c)
    arrived(xr, r_x)
    arrived(sr, r_s)
    one, two = sr[0].reshape(NT, HD), sr[1].reshape(NT, HD)
    top = jnp.maximum(one, two)
    part1 = pltpu.roll(one, HD // 2, 1) * jnp.exp2((one - top) * SCALE2)
    part2 = pltpu.roll(two, HD // 2, 1) * jnp.exp2((two - top) * SCALE2)
    whole = part1 + part2
    shares = jnp.concatenate(
        [part1 / whole, part2 / whole, jnp.zeros((HD - 2 * NT, HD), jnp.float32)], axis=0
    ).T
    for src in range(NT):
        for h in range(NH):
            rows = slice(h * CHUNK, (h + 1) * CHUNK)
            joined = xr[0, h, src].astype(jnp.float32) * shares[rows, src : src + 1]
            joined += xr[1, h, src].astype(jnp.float32) * shares[rows, NT + src : NT + src + 1]
            joined += cr[src, :, h * HD : (h + 1) * HD].astype(jnp.float32)
            lo = (src * NH + h) * HD
            out_ref[:, lo : lo + HD] = joined.astype(jnp.bfloat16)

    assert counts["bytes"] == SENT * 512 and counts["r"] <= RECVS, counts
    pltpu.make_async_copy(tally, tally, ssem.at[0]).wait()


def local(q_self, k_self, v_self, q_cross, k_text, v_text, text_len, timestep, gate_table):
    bf16, f32 = jnp.bfloat16, jnp.float32
    smem = pl.BlockSpec(memory_space=pltpu.SMEM)
    vmem = pl.BlockSpec(memory_space=pltpu.VMEM)
    hbm = pl.BlockSpec(memory_space=pltpu.HBM)
    return pl.pallas_call(
        kernel,
        out_shape=jax.ShapeDtypeStruct((CHUNK, NT * NH * HD), bf16),
        in_specs=[smem, smem, hbm, hbm, hbm, hbm, hbm, hbm, hbm],
        out_specs=vmem,
        scratch_shapes=[
            pltpu.VMEM((NH, NY, NX, ROWS, HD), bf16),
            pltpu.VMEM((NH, NY, NX, ROWS, HD), bf16),
            pltpu.VMEM((NH, 4, ROWS, HD), bf16),
            pltpu.VMEM((2, NH, ROWS // 2, HD), bf16),
            pltpu.VMEM((ROWS, NH * HD), bf16),
            pltpu.VMEM(gate_table.shape, f32),
            pltpu.VMEM((1, NH * HD), f32),
            pltpu.VMEM(k_text.shape, bf16),
            pltpu.VMEM(v_text.shape, bf16),
            pltpu.VMEM((2, 8, NH * HD), f32),
            pltpu.VMEM((8, NH * HD), f32),
            pltpu.VMEM((2, NY * NX, 16, NH * HD), bf16),
            pltpu.VMEM((NH, 4, HD + 8, ROWS), f32),
            pltpu.VMEM((NH, 2, HD + 8, ROWS), f32),
            pltpu.VMEM((2, NT, HD), f32),
            pltpu.VMEM((2, NH, NT, CHUNK, HD), bf16),
            pltpu.VMEM((2, NT, 1, HD), f32),
            pltpu.VMEM((2, NH, NT, CHUNK, HD), bf16),
            pltpu.VMEM((2, NT, 1, HD), f32),
            pltpu.VMEM((NT, CHUNK, NH * HD), bf16),
            pltpu.VMEM((NT, CHUNK, NH * HD), bf16),
            pltpu.VMEM((SENT, HD), f32),
            pltpu.SemaphoreType.DMA((1,)),
            pltpu.SemaphoreType.DMA((RECVS,)),
            pltpu.SemaphoreType.DMA((5,)),
            pltpu.SemaphoreType.REGULAR,
            pltpu.SemaphoreType.REGULAR,
        ],
        compiler_params=pltpu.CompilerParams(
            collective_id=0, has_side_effects=True, vmem_limit_bytes=64 * 1024 * 1024
        ),
        name="gated_attention",
    )(text_len, timestep, q_self, k_self, v_self, q_cross, k_text, v_text, gate_table)


def solution(mesh):
    placed = (
        P("ctx", "tp"),
        P("ctx", "tp"),
        P("ctx", "tp"),
        P("ctx", "tp"),
        P("ctx", "tp"),
        P("ctx", "tp"),
        P(),
        P(),
        P(None, "tp"),
    )
    return jax.shard_map(
        local, mesh=mesh, in_specs=placed, out_specs=P(("ctx", "tp"), None), check_vma=False
    )
```
